32 devices in a mesh: ctx: 8 (over y, x, core), fsdp: 4 (over z).
Axes of the slice: x: 2, y: 2, z: 4, core: 2. Of those that a mesh axis runs over, the one named last changes fastest.
Arguments:
- hidden: bfloat16 [4, 2048, 4096], P('fsdp', 'ctx'), may hold values from -6 to 6
- queries: bfloat16 [4, 2048, 2048], P('fsdp', 'ctx'), may hold values from -6 to 6
- key_weight: bfloat16 [4096, 512], P('fsdp'), may hold values from -0.09375 to 0.09375
- value_weight: bfloat16 [4096, 512], P('fsdp'), may hold values from -0.09375 to 0.09375
- key_gain: float32 [128], replicated, may hold values from 0.7 to 1.3
- head_scale: float32 [16], replicated, may hold values from 1 to 4
- block_mask: int32 [4, 16, 16], P('fsdp', 'ctx'), may hold values from 0 to 1, as said below
Outputs:
- attended: bfloat16 [4, 2048, 2048], P('fsdp', 'ctx')
The draws below stay inside these ranges and needn't reach their ends.
Inputs may be any that keep to these rules, and one draw needn't show every extreme that they name: `block_mask`: in each sequence's table, entry (q, k) is 1 where k == q, 0 where k > q, and either 0 or 1 where k < q.
All inputs are finite; a program needn't handle non-finite values.
Results may differ from the reference program's by a relative error of at most 0.011.
Values may be sent and summed in bfloat16 or wider, within the bound.
A program may use at most 64 MiB of HBM per device.

```python
import math
import jax
import jax.numpy as jnp
from jax import lax

D = 4096
HQ = 16
KVH = 4
HD = 128
BLOCK = 128
SEQ = 2048
BATCH = 4
NB = 16


def draw_block_mask(key, part):
    coin = jax.random.randint(key, (BATCH, NB, NB), 0, 2).astype(jnp.int32)
    query_index = lax_iota_rows()
    key_index = query_index.T
    below = (key_index < query_index).astype(jnp.int32)
    same = (key_index == query_index).astype(jnp.int32)
    return (coin * below[None] + same[None]).astype(jnp.int32)


def lax_iota_rows():
    column = jnp.arange(NB, dtype=jnp.int32)
    return jnp.broadcast_to(column[:, None], (NB, NB))


def level_of(stream_key, shape, pieces, smallest, largest):
    gain, own = 1.0, jax.random.fold_in(stream_key, 6)
    for position, parts in pieces:
        steps = jnp.exp(jax.random.uniform(jax.random.fold_in(own, position), (parts,), jnp.float32, smallest / len(pieces), largest / len(pieces)))
        gain = gain * jnp.repeat(steps, shape[position] // parts).reshape([-1 if axis == position else 1 for axis in range(len(shape))])
    return gain


def scatter_about(key, dims, deviation, reach, split=(), held_as=jnp.bfloat16):
    drawn = deviation * jax.random.normal(key, dims, jnp.float32)
    if split:
        drawn = drawn * level_of(key, dims, split, -0.22, 0.18)
    return jnp.clip(drawn, -reach, reach).astype(held_as)


def setup_inputs(seed: int = 0) -> dict:
    seeds = jax.random.split(jax.random.key(seed), 8)
    return {
        "hidden": scatter_about(seeds[0], (BATCH, SEQ, D), 1.0, 6.0, ((0, 4), (1, 8))),
        "queries": scatter_about(seeds[1], (BATCH, SEQ, HQ * HD), 1.0, 6.0, ((0, 4), (1, 8))),
        "key_weight": scatter_about(seeds[2], (D, KVH * HD), D ** -0.5, 0.09375, ((0, 4),)),
        "value_weight": scatter_about(seeds[3], (D, KVH * HD), D ** -0.5, 0.09375, ((0, 4),)),
        "key_gain": jnp.clip(1.0 + 0.06 * jax.random.normal(seeds[4], (HD,), jnp.float32), 0.7, 1.3),
        "head_scale": jnp.clip(jnp.exp(jax.random.uniform(seeds[5], (HQ,), jnp.float32, math.log(1.0), math.log(4.0))), 1.0, 4.0),
        "block_mask": draw_block_mask(jax.random.fold_in(seeds[7], 71), 0),
    }


def rms_scale(vecs):
    return vecs * lax.rsqrt(lax.optimization_barrier(jnp.mean(vecs * vecs, axis=-1, keepdims=True)) + 1e-06)

def reference(hidden, queries, key_weight, value_weight, key_gain, head_scale, block_mask):
    groups = HQ // KVH
    head_factor = (head_scale / math.sqrt(HD)).reshape(1, KVH, groups, 1)

    def one_sequence(inputs):
        seq_rows, query_rows, allow_table = inputs
        key_vecs = jnp.dot(seq_rows, key_weight, preferred_element_type=jnp.float32).reshape(SEQ, KVH, HD)
        key_vecs = (rms_scale(key_vecs) * key_gain).astype(jnp.bfloat16)
        value_vecs = jnp.dot(seq_rows, value_weight, preferred_element_type=jnp.float32).astype(jnp.bfloat16).reshape(SEQ, KVH, HD)
        scaled_q = (rms_scale(query_rows.astype(jnp.float32).reshape(SEQ, KVH, groups, HD)) * head_factor).astype(jnp.bfloat16)
        allowed = jnp.repeat(jnp.repeat(allow_table, BLOCK, axis=0), BLOCK, axis=1) > 0

        def one_head(head_inputs):
            query_head, key_head, value_head = head_inputs
            scores = jnp.einsum('qgd,kd->gqk', query_head.astype(jnp.float32), key_head.astype(jnp.float32))
            weights = jnp.where(allowed[None], jnp.exp(scores), jnp.float32(0.0))
            total = lax.optimization_barrier(jnp.sum(weights, axis=-1))
            rounded = weights.astype(jnp.bfloat16).astype(jnp.float32)
            mixed = jnp.einsum('gqk,kd->gqd', rounded, value_head.astype(jnp.float32))
            return (mixed / total[..., None]).astype(jnp.bfloat16)
        per_head = lax.map(one_head, (scaled_q.transpose(1, 0, 2, 3), key_vecs.transpose(1, 0, 2), value_vecs.transpose(1, 0, 2)))
        return per_head.transpose(2, 0, 1, 3).reshape(SEQ, HQ * HD)
    return lax.map(one_sequence, (hidden, queries, block_mask))
```

```python
import functools
import math

import jax
import jax.numpy as jnp
from jax import lax
from jax.experimental import pallas as pl
from jax.experimental.pallas import tpu as pltpu
from jax.sharding import PartitionSpec as P

MESH = pl.DeviceIdType.MESH


def flip(value, mask):
    bit = 1
    while bit <= mask:
        if mask & bit:
            value = value + bit - 2 * bit * lax.rem(lax.div(value, bit), 2)
        bit *= 2
    return value


def kernel(
    n_fsdp, n_chips, groups, hs_ref, mask_ref, gain_ref, hid_in, q_in, kw_in, vw_in, out_ref,
    wbuf, hid, qraw, qs, kvb, psum, acc, obuf, mbuf,
    loc_sem, sib_s, sib_r, zs, zr, xs, xr, ys, yr, fxs, fxr, fys, fyr, ks, kr,
):
    n_y = n_chips // 2
    tokens, width = hid_in.shape
    depth = kw_in.shape[0]
    half = kw_in.shape[1] // 2
    head = gain_ref.shape[1]
    frames, n_key_frames = mask_ref.shape
    frame = tokens // frames
    chip_rows = 2 * tokens
    chip_frames = 2 * frames
    kv_heads = half // head
    q_half = q_in.shape[1] // 2
    quarter = depth // n_chips

    z = lax.axis_index("fsdp")
    spot = lax.axis_index("ctx")
    chip = lax.div(spot, 2)
    core = lax.rem(spot, 2)
    y = lax.div(chip, 2)
    x = lax.rem(chip, 2)
    sibling = 1 - core

    def dev(to_chip, to_core, to_z):
        return (to_chip * 2 + to_core, to_z)

    x_chip = y * 2 + 1 - x

    def y_chip(k, column=None):
        return lax.rem(y + k, n_y) * 2 + (x if column is None else column)

    me_sib = dev(chip, sibling, z)
    x_dev = dev(x_chip, core, z)

    own_rows = pl.ds(pl.multiple_of(core * tokens, tokens), tokens)
    sib_rows = pl.ds(pl.multiple_of(sibling * tokens, tokens), tokens)
    own_half = pl.ds(pl.multiple_of(core * half, half), half)
    own_q = pl.ds(pl.multiple_of(core * q_half, q_half), q_half)
    sib_q = pl.ds(pl.multiple_of(sibling * q_half, q_half), q_half)

    local = [
        pltpu.make_async_copy(hid_in, hid.at[own_rows, :], loc_sem.at[0]),
        pltpu.make_async_copy(q_in.at[:, own_q], qraw.at[own_rows, :], loc_sem.at[1]),
        pltpu.make_async_copy(kw_in.at[:, own_half], wbuf.at[z, 0], loc_sem.at[2]),
        pltpu.make_async_copy(vw_in.at[:, own_half], wbuf.at[z, 1], loc_sem.at[3]),
    ]
    for copy in local:
        copy.start()

    partners = [me_sib]
    partners += [dev(chip, core, flip(z, j)) for j in range(1, n_fsdp)]
    partners += [dev(lax.rem(chip + d, n_chips), core, z) for d in range(1, n_chips)]
    barrier = pltpu.get_barrier_semaphore()
    for partner in partners:
        pl.semaphore_signal(barrier, inc=1, device_id=partner, device_id_type=MESH)
    for f in range(frames):
        for k in range(n_key_frames):
            seen = jnp.where(mask_ref[f, k] > 0, 1.0, 0.0).astype(jnp.float32)
            mbuf[core, f, pl.ds(k, 1), :] = jnp.full((1, head), seen, jnp.float32)
    pl.semaphore_wait(barrier, len(partners))

    def remote(src, dst, send, recv, to):
        return pltpu.make_async_remote_copy(
            src_ref=src, dst_ref=dst, send_sem=send, recv_sem=recv, device_id=to, device_id_type=MESH
        )

    def rows_of(q, part=None):
        if part is None:
            return pl.ds(pl.multiple_of(q * quarter, quarter), quarter)
        size = quarter // 2
        return pl.ds(pl.multiple_of(q * quarter + part * size, size), size)

    def piece(j, kv, q, part=None):
        return wbuf.at[flip(z, j), kv, rows_of(q, part), :]

    def z_copy(kv, j):
        source = (kw_in, vw_in)[kv].at[rows_of(chip), own_half]
        landing = wbuf.at[z, kv, rows_of(chip), :]
        return remote(source, landing, zs.at[kv, j], zr.at[kv, j], dev(chip, core, flip(z, j)))

    def z_land(kv, j):
        land = piece(j, kv, chip)
        return remote(land, land, zs.at[kv, j], zr.at[kv, j], dev(chip, core, flip(z, j)))

    def x_copy(kv, j, q):
        land = piece(j, kv, q)
        return remote(land, land, xs.at[kv, j], xr.at[kv, j], x_dev)

    def y_copy(kv, j, k, q):
        land = piece(j, kv, q)
        return remote(land, land, ys.at[kv, j, k], yr.at[kv, j, k], dev(y_chip(k), core, z))

    def fx_copy(kv, j, k, q):
        land = piece(j, kv, q, 0)
        return remote(land, land, fxs.at[kv, j, k], fxr.at[kv, j, k], x_dev)

    def fy_copy(kv, j, k, q):
        land = piece(j, kv, q, 1)
        return remote(land, land, fys.at[kv, j, k], fyr.at[kv, j, k], dev(y_chip(k), core, z))

    others = list(range(1, n_fsdp))
    back = lambda k: n_y - k
    waits = []

    def go(copy):
        copy.start()
        waits.append(copy)

    for kv in range(2):
        for j in others:
            go(z_copy(kv, j))
        if kv == 0:
            sib = [
                remote(hid_in, hid.at[own_rows, :], sib_s.at[0], sib_r.at[0], me_sib),
                remote(q_in.at[:, sib_q], qraw.at[own_rows, :], sib_s.at[1], sib_r.at[1], me_sib),
                remote(mbuf.at[core], mbuf.at[core], sib_s.at[2], sib_r.at[2], me_sib),
            ]
            for copy in sib:
                go(copy)

    def sib_land(n):
        land = (hid.at[sib_rows, :], qraw.at[sib_rows, :], mbuf.at[sibling])[n]
        return remote(land, land, sib_s.at[n], sib_r.at[n], me_sib)

    def stage1(kv, j):
        z_land(kv, j).wait_recv()
        go(x_copy(kv, j, chip))
        for k in range(1, n_y):
            go(y_copy(kv, j, k, chip))

    def stage2(kv, j):
        x_copy(kv, j, x_chip).wait_recv()
        for k in range(1, n_y):
            go(fy_copy(kv, j, k, x_chip))
        for k in range(1, n_y):
            source = y_chip(back(k))
            y_copy(kv, j, k, source).wait_recv()
            go(fx_copy(kv, j, k, source))

    def multiply(kv, j, first):
        zz = flip(z, j)
        cols = pl.ds(pl.multiple_of(zz * depth, depth), depth)
        part = jnp.dot(hid[:, cols], wbuf[zz, kv], preferred_element_type=jnp.float32)
        if first:
            psum[...] = part
        else:
            psum[...] += part

    def stage3(kv, j):
        for k in range(1, n_y):
            source = y_chip(back(k), 1 - x)
            fx_copy(kv, j, k, source).wait_recv()
            fy_copy(kv, j, k, source).wait_recv()
        multiply(kv, j, False)

    def kv_copy(kv, d, to):
        return remote(kvb.at[chip, kv], kvb.at[chip, kv], ks.at[kv, d], kr.at[kv, d], dev(to, core, z))

    def send_kv(kv):
        for d in range(1, n_chips):

            @pl.when(chip + d < n_chips)
            def _():
                kv_copy(kv, d, chip + d).start()

    for copy in local:
        copy.wait()
    for n in range(3):
        sib_land(n).wait_recv()

    def scale_queries(h, carried):
        kv_head = lax.div(h, groups)
        g = lax.rem(h, groups)
        factor = hs_ref[core * (kv_heads * groups) + h] * (1.0 / math.sqrt(head))
        cols = pl.ds(pl.multiple_of(h * head, head), head)
        for f in range(chip_frames):
            q = qraw[f * frame : (f + 1) * frame, cols].astype(jnp.float32)
            mean = jnp.mean(q * q, axis=-1, keepdims=True)
            q = q * lax.rsqrt(mean + 1e-6) * factor
            qs[kv_head, f, pl.ds(pl.multiple_of(g * frame, frame), frame), :] = q.astype(jnp.bfloat16)
        return carried

    def finish(kv):
        for h in range(kv_heads):
            vecs = psum[:, h * head : (h + 1) * head]
            if kv == 0:
                mean = jnp.mean(vecs * vecs, axis=-1, keepdims=True)
                vecs = vecs * lax.rsqrt(mean + 1e-6) * gain_ref[...]
            kvb[chip, kv, h] = vecs.astype(jnp.bfloat16)
        send_kv(kv)

    units = [(kv, j) for kv in range(2) for j in others]
    multiply(0, 0, True)
    for t in range(len(units) + 2):
        if t < len(units):
            stage1(*units[t])
        if t == 0:
            lax.fori_loop(0, kv_heads * groups, scale_queries, 0)
        if 0 <= t - 1 < len(units):
            stage2(*units[t - 1])
        if t >= 2:
            stage3(*units[t - 2])
            if t - 2 == len(others) - 1:
                finish(0)
                multiply(1, 0, True)
    finish(1)

    def attend(source, first):
        def body(step, carried):
            h = lax.div(step, chip_frames)
            f = lax.rem(step, chip_frames)
            scores = lax.dot_general(
                qs[h, f], kvb[source, 0, h], (((1,), (1,)), ((), ())), preferred_element_type=jnp.float32
            )
            weights = jnp.exp(scores).astype(jnp.bfloat16)
            values = []
            for k in range(chip_frames):
                seen = mbuf[lax.div(f, frames), lax.rem(f, frames), pl.ds(source * chip_frames + k, 1), :]
                seen = jnp.broadcast_to(seen, (frame, head)).astype(jnp.bfloat16)
                value = kvb[source, 1, h, k * frame : (k + 1) * frame, :] * seen
                values.append(jnp.concatenate([value, seen], axis=1))
            both = jnp.dot(weights, jnp.concatenate(values, axis=0), preferred_element_type=jnp.float32)
            if first:
                acc[step] = both
            else:
                acc[step] += both
            return carried

        lax.fori_loop(0, kv_heads * chip_frames, body, 0)

    attend(chip, True)
    for d in range(1, n_chips):

        @pl.when(chip >= d)
        def _():
            source = chip - d
            for kv in range(2):
                land = kvb.at[source, kv]
                remote(land, land, ks.at[kv, d], kr.at[kv, d], me_sib).wait_recv()
            attend(source, False)

    def divide(f, carried):
        for h in range(kv_heads):
            both = acc[h * chip_frames + f]
            ratio = (both[:, :head] / both[:, head:]).astype(jnp.bfloat16)
            for g in range(groups):
                at = (h * groups + g) * head
                obuf[pl.ds(pl.multiple_of(f * frame, frame), frame), at : at + head] = ratio[
                    g * frame : (g + 1) * frame
                ]
        return carried

    lax.fori_loop(0, chip_frames, divide, 0)
    keep = pltpu.make_async_copy(obuf.at[own_rows, :], out_ref.at[:, own_q], loc_sem.at[4])
    give = remote(obuf.at[sib_rows, :], out_ref.at[:, own_q], sib_s.at[3], sib_r.at[3], me_sib)
    keep.start()
    give.start()

    for copy in waits:
        copy.wait_send()
    for kv in range(2):
        for d in range(1, n_chips):

            @pl.when(chip + d < n_chips)
            def _():
                kv_copy(kv, d, chip + d).wait_send()

    keep.wait()
    give.wait_send()
    remote(out_ref.at[:, sib_q], out_ref.at[:, sib_q], sib_s.at[3], sib_r.at[3], me_sib).wait_recv()


def shards(hidden, queries, key_weight, value_weight, key_gain, head_scale, block_mask):
    n_fsdp = lax.axis_size("fsdp")
    n_chips = lax.axis_size("ctx") // 2
    n_y = n_chips // 2
    _, tokens, width = hidden.shape
    q_width = queries.shape[2]
    depth, kv_width = key_weight.shape
    head = key_gain.shape[0]
    heads = head_scale.shape[0]
    half = kv_width // 2
    kv_heads = half // head
    groups = heads // (2 * kv_heads)
    frames, n_key_frames = block_mask.shape[1:]
    frame = tokens // frames
    hbm = pl.BlockSpec(memory_space=pl.ANY)
    smem = pl.BlockSpec(memory_space=pltpu.SMEM)
    dma = pltpu.SemaphoreType.DMA
    out = pl.pallas_call(
        functools.partial(kernel, n_fsdp, n_chips, groups),
        out_shape=jax.ShapeDtypeStruct((tokens, q_width), jnp.bfloat16),
        in_specs=[smem, smem, pl.BlockSpec(memory_space=pltpu.VMEM), hbm, hbm, hbm, hbm],
        out_specs=hbm,
        scratch_shapes=[
            pltpu.VMEM((n_fsdp, 2, depth, half), jnp.bfloat16),
            pltpu.VMEM((2 * tokens, width), jnp.bfloat16),
            pltpu.VMEM((2 * tokens, q_width // 2), jnp.bfloat16),
            pltpu.VMEM((kv_heads, 2 * frames, groups * frame, head), jnp.bfloat16),
            pltpu.VMEM((n_chips, 2, kv_heads, 2 * tokens, head), jnp.bfloat16),
            pltpu.VMEM((2 * tokens, half), jnp.float32),
            pltpu.VMEM((kv_heads * 2 * frames, groups * frame, 2 * head), jnp.float32),
            pltpu.VMEM((2 * tokens, q_width // 2), jnp.bfloat16),
            pltpu.VMEM((2, frames, n_key_frames, head), jnp.float32),
            dma((5,)),
            dma((4,)),
            dma((4,)),
            dma((2, n_fsdp)),
            dma((2, n_fsdp)),
            dma((2, n_fsdp)),
            dma((2, n_fsdp)),
            dma((2, n_fsdp, n_y)),
            dma((2, n_fsdp, n_y)),
            dma((2, n_fsdp, n_y)),
            dma((2, n_fsdp, n_y)),
            dma((2, n_fsdp, n_y)),
            dma((2, n_fsdp, n_y)),
            dma((2, n_chips)),
            dma((2, n_chips)),
        ],
        compiler_params=pltpu.CompilerParams(
            collective_id=0, has_side_effects=True, vmem_limit_bytes=48 * 1024 * 1024
        ),
    )(
        head_scale, block_mask[0], key_gain.reshape(1, head), hidden[0], queries[0], key_weight, value_weight
    )
    return out[None]


def solution(mesh):
    placed = (
        P("fsdp", "ctx", None),
        P("fsdp", "ctx", None),
        P("fsdp", None),
        P("fsdp", None),
        P(),
        P(),
        P("fsdp", "ctx", None),
    )
    return jax.shard_map(
        shards, mesh=mesh, in_specs=placed, out_specs=P("fsdp", "ctx", None), check_vma=False
    )
```

```python
import functools
import math

import jax
import jax.numpy as jnp
from jax import lax
from jax.experimental import pallas as pl
from jax.experimental.pallas import tpu as pltpu
from jax.sharding import PartitionSpec as P

MESH = pl.DeviceIdType.MESH


DIAGONAL_ALONG_Z = (False, False)


def kernel(
    n_fsdp, n_chips, groups, hs_ref, mask_ref, gain_ref, hid_in, q_in, kw_in, vw_in, out_ref,
    wbuf, hid, qraw, qs, kvb, psum, pbuf, acc, obuf, mbuf,
    loc_sem, sib_s, sib_r, zs, zr, xs, xr, ys, yr, fxs, fxr, fys, fyr, ks, kr,
):
    n_y = n_chips // 2
    tokens, width = hid_in.shape
    depth = kw_in.shape[0]
    half = kw_in.shape[1] // 2
    head = gain_ref.shape[1]
    frames, n_key_frames = mask_ref.shape
    frame = tokens // frames
    chip_rows = 2 * tokens
    chip_frames = 2 * frames
    kv_heads = half // head
    q_half = q_in.shape[1] // 2
    quarter = depth // n_chips

    z = lax.axis_index("fsdp")
    spot = lax.axis_index("ctx")
    chip = lax.div(spot, 2)
    core = lax.rem(spot, 2)
    y = lax.div(chip, 2)
    x = lax.rem(chip, 2)
    sibling = 1 - core

    def dev(to_chip, to_core, to_z):
        return (to_chip * 2 + to_core, to_z)

    x_chip = y * 2 + 1 - x

    def y_chip(k, column=None):
        return lax.rem(y + k, n_y) * 2 + (x if column is None else column)

    me_sib = dev(chip, sibling, z)
    x_dev = dev(x_chip, core, z)

    own_rows = pl.ds(pl.multiple_of(core * tokens, tokens), tokens)
    sib_rows = pl.ds(pl.multiple_of(sibling * tokens, tokens), tokens)
    own_half = pl.ds(pl.multiple_of(core * half, half), half)
    own_q = pl.ds(pl.multiple_of(core * q_half, q_half), q_half)
    sib_q = pl.ds(pl.multiple_of(sibling * q_half, q_half), q_half)

    local = [
        pltpu.make_async_copy(hid_in, hid.at[own_rows, :], loc_sem.at[0]),
        pltpu.make_async_copy(q_in.at[:, own_q], qraw.at[own_rows, :], loc_sem.at[1]),
        pltpu.make_async_copy(kw_in.at[:, own_half], wbuf.at[z, 0], loc_sem.at[2]),
        pltpu.make_async_copy(vw_in.at[:, own_half], wbuf.at[z, 1], loc_sem.at[3]),
    ]
    for copy in local:
        copy.start()

    partners = [me_sib]
    partners += [dev(chip, core, lax.rem(z + j, n_fsdp)) for j in range(1, n_fsdp)]
    partners += [dev(lax.rem(chip + d, n_chips), core, z) for d in range(1, n_chips)]
    barrier = pltpu.get_barrier_semaphore()
    for partner in partners:
        pl.semaphore_signal(barrier, inc=1, device_id=partner, device_id_type=MESH)

    def has_next(up):
        return z + 1 < n_fsdp if up else z >= 1

    def has_unit(up, d):
        return z >= d if up else z + d < n_fsdp

    def next_dev(up):
        return dev(chip, core, z + 1 if up else z - 1)

    for f in range(frames):
        for k in range(n_key_frames):
            seen = jnp.where(mask_ref[f, k] > 0, 1.0, 0.0).astype(jnp.float32)
            mbuf[core, f, pl.ds(k, 1), :] = jnp.full((1, head), seen, jnp.float32)
    pl.semaphore_wait(barrier, len(partners))

    def remote(src, dst, send, recv, to):
        return pltpu.make_async_remote_copy(
            src_ref=src, dst_ref=dst, send_sem=send, recv_sem=recv, device_id=to, device_id_type=MESH
        )

    def rows_of(q, part=None):
        if part is None:
            return pl.ds(pl.multiple_of(q * quarter, quarter), quarter)
        size = quarter // 2
        return pl.ds(pl.multiple_of(q * quarter + part * size, size), size)

    def piece(zz, kv, q, part=None):
        return wbuf.at[zz, kv, rows_of(q, part), :]

    back = lambda k: n_y - k

    def z_parts(kv):
        quarters = [chip]
        if DIAGONAL_ALONG_Z[kv]:
            quarters += [y_chip(k, 1 - x) for k in range(1, n_y)]
        return list(enumerate(quarters))

    def z_copy(kv, zz, n, q, up, first=False):
        land = piece(zz, kv, q)
        source = (kw_in, vw_in)[kv].at[rows_of(q), own_half] if first else land
        return remote(source, land, zs.at[up, kv, zz, n], zr.at[kv, zz, n], next_dev(up))

    def x_copy(kv, zz, q):
        land = piece(zz, kv, q)
        return remote(land, land, xs.at[kv, zz], xr.at[kv, zz], x_dev)

    def y_copy(kv, zz, k, q):
        land = piece(zz, kv, q)
        return remote(land, land, ys.at[kv, zz, k], yr.at[kv, zz, k], dev(y_chip(k), core, z))

    def fx_copy(kv, zz, k, q):
        land = piece(zz, kv, q, 0)
        return remote(land, land, fxs.at[kv, zz, k], fxr.at[kv, zz, k], x_dev)

    def fy_copy(kv, zz, k, q):
        land = piece(zz, kv, q, 1)
        return remote(land, land, fys.at[kv, zz, k], fyr.at[kv, zz, k], dev(y_chip(k), core, z))

    def first_send(kv):
        for up in (True, False):

            @pl.when(has_next(up))
            def _():
                for n, q in z_parts(kv):
                    z_copy(kv, z, n, q, int(up), True).start()

    first_send(0)
    sib = [
        remote(hid_in, hid.at[own_rows, :], sib_s.at[0], sib_r.at[0], me_sib),
        remote(q_in.at[:, sib_q], qraw.at[own_rows, :], sib_s.at[1], sib_r.at[1], me_sib),
        remote(mbuf.at[core], mbuf.at[core], sib_s.at[2], sib_r.at[2], me_sib),
    ]
    for copy in sib:
        copy.start()

    def sib_land(n):
        land = (hid.at[sib_rows, :], qraw.at[sib_rows, :], mbuf.at[sibling])[n]
        return remote(land, land, sib_s.at[n], sib_r.at[n], me_sib)

    def each_unit(d, action):
        for up in (True, False):

            @pl.when(has_unit(up, d))
            def _():
                action(up, z - d if up else z + d)

    def stage1(kv, d):
        def action(up, zz):
            for n, q in z_parts(kv):
                z_copy(kv, zz, n, q, int(up)).wait_recv()

                @pl.when(has_next(up))
                def _():
                    z_copy(kv, zz, n, q, int(up)).start()

                if n == 0:
                    x_copy(kv, zz, chip).start()
                    for k in range(1, n_y):
                        y_copy(kv, zz, k, chip).start()

        each_unit(d, action)

    def stage2(kv, d):
        def action(up, zz):
            x_copy(kv, zz, x_chip).wait_recv()
            if not DIAGONAL_ALONG_Z[kv]:
                for k in range(1, n_y):
                    fy_copy(kv, zz, k, x_chip).start()
            for k in range(1, n_y):
                source = y_chip(back(k))
                y_copy(kv, zz, k, source).wait_recv()
                if not DIAGONAL_ALONG_Z[kv]:
                    fx_copy(kv, zz, k, source).start()

        each_unit(d, action)

    def multiply(kv, zz, first):
        cols = pl.ds(pl.multiple_of(zz * depth, depth), depth)
        part = jnp.dot(hid[:, cols], wbuf[zz, kv], preferred_element_type=jnp.float32)
        if first:
            psum[...] = part
        else:
            psum[...] += part

    def stage3(kv, d):
        def action(up, zz):
            if not DIAGONAL_ALONG_Z[kv]:
                for k in range(1, n_y):
                    source = y_chip(back(k), 1 - x)
                    fx_copy(kv, zz, k, source).wait_recv()
                    fy_copy(kv, zz, k, source).wait_recv()
            multiply(kv, zz, False)

        each_unit(d, action)

    def finish_sends():
        for copy in sib:
            copy.wait_send()
        for kv in range(2):
            for up in (True, False):

                @pl.when(has_next(up))
                def _():
                    for n, q in z_parts(kv):
                        z_copy(kv, z, n, q, int(up), True).wait_send()

            def action(up, zz):
                for n, q in z_parts(kv):

                    @pl.when(has_next(up))
                    def _():
                        z_copy(kv, zz, n, q, int(up)).wait_send()

                x_copy(kv, zz, chip).wait_send()
                for k in range(1, n_y):
                    y_copy(kv, zz, k, chip).wait_send()
                    if not DIAGONAL_ALONG_Z[kv]:
                        fy_copy(kv, zz, k, x_chip).wait_send()
                        fx_copy(kv, zz, k, y_chip(back(k))).wait_send()

            for d in range(1, n_fsdp):
                each_unit(d, action)

    def kv_copy(kv, d, to):
        return remote(kvb.at[chip, kv], kvb.at[chip, kv], ks.at[kv, d], kr.at[kv, d], dev(to, core, z))

    def send_kv(kv):
        for d in range(1, n_chips):

            @pl.when(chip + d < n_chips)
            def _():
                kv_copy(kv, d, chip + d).start()

    for copy in local:
        copy.wait()
    for n in range(3):
        sib_land(n).wait_recv()

    def scale_queries(h, carried):
        kv_head = lax.div(h, groups)
        g = lax.rem(h, groups)
        factor = hs_ref[core * (kv_heads * groups) + h] * (1.0 / math.sqrt(head))
        cols = pl.ds(pl.multiple_of(h * head, head), head)
        for f in range(chip_frames):
            q = qraw[f * frame : (f + 1) * frame, cols].astype(jnp.float32)
            mean = jnp.mean(q * q, axis=-1, keepdims=True)
            q = q * lax.rsqrt(mean + 1e-6) * factor
            qs[kv_head, f, pl.ds(pl.multiple_of(g * frame, frame), frame), :] = q.astype(jnp.bfloat16)
        return carried

    def finish(kv):
        for h in range(kv_heads):
            vecs = psum[:, h * head : (h + 1) * head]
            if kv == 0:
                mean = jnp.mean(vecs * vecs, axis=-1, keepdims=True)
                vecs = vecs * lax.rsqrt(mean + 1e-6) * gain_ref[...]
            kvb[chip, kv, h] = vecs.astype(jnp.bfloat16)
        send_kv(kv)

    def score(source):
        def body(step, carried):
            h = lax.div(step, chip_frames)
            f = lax.rem(step, chip_frames)
            scores = lax.dot_general(
                qs[h, f], kvb[source, 0, h], (((1,), (1,)), ((), ())), preferred_element_type=jnp.float32
            )
            pbuf[source, step] = jnp.exp(scores).astype(jnp.bfloat16)
            return carried

        lax.fori_loop(0, kv_heads * chip_frames, body, 0, unroll=2)

    def mix(source, first):
        def body(step, carried):
            h = lax.div(step, chip_frames)
            f = lax.rem(step, chip_frames)
            values = []
            for k in range(chip_frames):
                seen = mbuf[lax.div(f, frames), lax.rem(f, frames), pl.ds(source * chip_frames + k, 1), :]
                seen = jnp.broadcast_to(seen, (frame, head)).astype(jnp.bfloat16)
                value = kvb[source, 1, h, k * frame : (k + 1) * frame, :] * seen
                values.append(jnp.concatenate([value, seen], axis=1))
            both = jnp.dot(
                pbuf[source, step], jnp.concatenate(values, axis=0), preferred_element_type=jnp.float32
            )
            if first:
                acc[step] = both
            else:
                acc[step] += both
            return carried

        lax.fori_loop(0, kv_heads * chip_frames, body, 0, unroll=2)

    def with_piece(kv, use, among=True):
        for d in range(1, n_chips):

            @pl.when(jnp.logical_and(chip >= d, among))
            def _():
                source = chip - d
                land = kvb.at[source, kv]
                remote(land, land, ks.at[kv, d], kr.at[kv, d], me_sib).wait_recv()
                use(source)

    units = [(kv, d) for kv in range(2) for d in range(1, n_fsdp)]
    last = len(units) - 1
    multiply(0, z, True)
    for t in range(len(units) + 2):
        if t <= last:
            stage1(*units[t])
        if t == 0:
            first_send(1)
            lax.fori_loop(0, kv_heads * groups, scale_queries, 0)
        if 0 <= t - 1 <= last:
            stage2(*units[t - 1])
        if t - 1 == last:
            with_piece(0, score, chip == n_chips - 1)
        if t >= 2:
            stage3(*units[t - 2])
            if t - 2 == n_fsdp - 2:
                finish(0)
                multiply(1, z, True)
                score(chip)
    finish(1)
    with_piece(0, score, chip < n_chips - 1)
    mix(chip, True)
    with_piece(1, lambda source: mix(source, False))

    def divide(f, carried):
        for h in range(kv_heads):
            both = acc[h * chip_frames + f]
            ratio = (both[:, :head] / both[:, head:]).astype(jnp.bfloat16)
            for g in range(groups):
                at = (h * groups + g) * head
                obuf[pl.ds(pl.multiple_of(f * frame, frame), frame), at : at + head] = ratio[
                    g * frame : (g + 1) * frame
                ]
        return carried

    lax.fori_loop(0, chip_frames, divide, 0)
    keep = pltpu.make_async_copy(obuf.at[own_rows, :], out_ref.at[:, own_q], loc_sem.at[4])
    give = remote(obuf.at[sib_rows, :], out_ref.at[:, own_q], sib_s.at[3], sib_r.at[3], me_sib)
    keep.start()
    give.start()

    finish_sends()
    for kv in range(2):
        for d in range(1, n_chips):

            @pl.when(chip + d < n_chips)
            def _():
                kv_copy(kv, d, chip + d).wait_send()

    keep.wait()
    give.wait_send()
    remote(out_ref.at[:, sib_q], out_ref.at[:, sib_q], sib_s.at[3], sib_r.at[3], me_sib).wait_recv()


def shards(hidden, queries, key_weight, value_weight, key_gain, head_scale, block_mask):
    n_fsdp = lax.axis_size("fsdp")
    n_chips = lax.axis_size("ctx") // 2
    n_y = n_chips // 2
    _, tokens, width = hidden.shape
    q_width = queries.shape[2]
    depth, kv_width = key_weight.shape
    head = key_gain.shape[0]
    heads = head_scale.shape[0]
    half = kv_width // 2
    kv_heads = half // head
    groups = heads // (2 * kv_heads)
    frames, n_key_frames = block_mask.shape[1:]
    frame = tokens // frames
    hbm = pl.BlockSpec(memory_space=pltpu.HBM)
    smem = pl.BlockSpec(memory_space=pltpu.SMEM)
    dma = pltpu.SemaphoreType.DMA
    out = pl.pallas_call(
        functools.partial(kernel, n_fsdp, n_chips, groups),
        out_shape=jax.ShapeDtypeStruct((tokens, q_width), jnp.bfloat16),
        in_specs=[smem, smem, pl.BlockSpec(memory_space=pltpu.VMEM), hbm, hbm, hbm, hbm],
        out_specs=hbm,
        scratch_shapes=[
            pltpu.VMEM((n_fsdp, 2, depth, half), jnp.bfloat16),
            pltpu.VMEM((2 * tokens, width), jnp.bfloat16),
            pltpu.VMEM((2 * tokens, q_width // 2), jnp.bfloat16),
            pltpu.VMEM((kv_heads, 2 * frames, groups * frame, head), jnp.bfloat16),
            pltpu.VMEM((n_chips, 2, kv_heads, 2 * tokens, head), jnp.bfloat16),
            pltpu.VMEM((2 * tokens, half), jnp.float32),
            pltpu.VMEM((n_chips, kv_heads * 2 * frames, groups * frame, 2 * tokens), jnp.bfloat16),
            pltpu.VMEM((kv_heads * 2 * frames, groups * frame, 2 * head), jnp.float32),
            pltpu.VMEM((2 * tokens, q_width // 2), jnp.bfloat16),
            pltpu.VMEM((2, frames, n_key_frames, head), jnp.float32),
            dma((5,)),
            dma((4,)),
            dma((4,)),
            dma((2, 2, n_fsdp, n_y)),
            dma((2, n_fsdp, n_y)),
            dma((2, n_fsdp)),
            dma((2, n_fsdp)),
            dma((2, n_fsdp, n_y)),
            dma((2, n_fsdp, n_y)),
            dma((2, n_fsdp, n_y)),
            dma((2, n_fsdp, n_y)),
            dma((2, n_fsdp, n_y)),
            dma((2, n_fsdp, n_y)),
            dma((2, n_chips)),
            dma((2, n_chips)),
        ],
        compiler_params=pltpu.CompilerParams(
            collective_id=0, has_side_effects=True, vmem_limit_bytes=63 * 1024 * 1024
        ),
    )(
        head_scale, block_mask[0], key_gain.reshape(1, head), hidden[0], queries[0], key_weight, value_weight
    )
    return out[None]


def solution(mesh):
    placed = (
        P("fsdp", "ctx", None),
        P("fsdp", "ctx", None),
        P("fsdp", None),
        P("fsdp", None),
        P(),
        P(),
        P("fsdp", "ctx", None),
    )
    return jax.shard_map(
        shards, mesh=mesh, in_specs=placed, out_specs=P("fsdp", "ctx", None), check_vma=False
    )
```
